32 devices in a mesh: dp: 2 (over x), expert: 16 (over z, y, core).
Axes of the slice: x: 2, y: 2, z: 4, core: 2. Of those that a mesh axis runs over, the one named last changes fastest.
Arguments:
- tokens: bfloat16 [4096, 3584], P(('dp', 'expert')), may hold values from -6 to 6
- cotangent: bfloat16 [4096, 3584], P(('dp', 'expert')), may hold values from -0.09375 to 0.09375
- expert_ids: int32 [4096, 8], P(('dp', 'expert')), may hold values from 0 to 255, all different within a row; in each aligned block of 128 rows (0 to 127, 128 to 255, ...) at most 6 rows name the same one
- gates: bfloat16 [4096, 8], P(('dp', 'expert')), may hold values from 0.049804688 to 1
- swap_flags: int32 [8], replicated, may hold values 0 or 1
- gate_w: bfloat16 [16, 3584, 1024], P('expert', None, 'dp'), may hold values from -0.09375 to 0.09375
- up_w: bfloat16 [16, 3584, 1024], P('expert', None, 'dp'), may hold values from -0.09375 to 0.09375
- down_w: bfloat16 [16, 1024, 3584], P('expert', 'dp'), may hold values from -0.1875 to 0.1875
Outputs:
- grad_gate_w: bfloat16 [16, 3584, 1024], P('expert', None, 'dp')
- grad_up_w: bfloat16 [16, 3584, 1024], P('expert', None, 'dp')
- grad_down_w: bfloat16 [16, 1024, 3584], P('expert', 'dp')
- score_grad: float32 [4096, 8], P(('dp', 'expert'))
The draws below stay inside these ranges and needn't reach their ends.
Inputs may be any that keep to these rules, and one draw needn't show every extreme that they name: `expert_ids`: among the 128 rows of one device no expert is named more than 6 times, a bound that some block reaches; the numbers of one row differ. `swap_flags`: 1 means that slots s and s + 8 trade their experts.
All inputs are finite; a program needn't handle non-finite values.
Results may differ from the reference program's by a relative error of at most 0.011.
Values may be sent and summed in bfloat16 or wider, within the bound.
No kernel may reach another device: no remote copies, remote signals or barrier semaphores. Data moves between devices by JAX's collectives and lax.ppermute only.
A program may use at most 128 MiB of HBM per device.

```python
import math
import jax
import jax.numpy as jnp
import numpy as np
from jax import lax

D = 3584
F = 1024
ALL_EXPERTS = 256
TOPK = 8
TOK_DEV = 128
CAP = 6
EXPERTS = 16
HALF = 8
TOKENS = 4096
N_DP = 2
N_EXPERT = 16


def with_ends(array, stream_key, least, largest):
    dims = array.shape
    index_at = [jax.random.randint(jax.random.fold_in(stream_key, axis), (), 0, dims[axis]) for axis in range(len(dims))]
    array = array.at[tuple(index_at)].set(least)
    longest = dims.index(max(dims))
    index_at[longest] = (index_at[longest] + 1) % dims[longest]
    return array.at[tuple(index_at)].set(largest)


def block_scale(key, extent, cuts, least, high):
    gain = 1.0
    for position, shards_of in cuts:
        draws = jax.random.uniform(jax.random.fold_in(jax.random.fold_in(key, 6), position), (shards_of,), jnp.float32, least / len(cuts), high / len(cuts))
        gain = gain * jnp.repeat(jnp.exp(draws), extent[position] // shards_of).reshape((-1,) + (1,) * (len(extent) - 1 - position))
    return gain


def assign_block(own_key, own, number, rows, amount, top, bound, skew):
    order = jax.random.permutation(own_key, amount)
    crowded, usual = shares(amount, rows * top, bound, skew, True), shares(amount, rows * top, bound, skew, False)
    places = jnp.arange(amount)

    def named(lengths, turn):
        used = int((lengths > 0).sum())
        fixed = max(1, used // 4)
        moved = fixed + (places - fixed + turn * (used - fixed)) % max(1, amount - fixed)
        return jnp.zeros((amount,), jnp.int32).at[order[jnp.where(places < fixed, places, moved)]].set(jnp.asarray(lengths, jnp.int32))

    lengths = jnp.where(number % 4 == 0, named(crowded, number // 4), named(usual, number - number // 4 - 1))
    mixed = jax.random.permutation(jax.random.fold_in(own, 3), amount)
    donor, taker = mixed[0:amount // 2 * 2:2], mixed[1:amount // 2 * 2:2]
    slack = jnp.minimum(lengths[donor] - 1, bound - lengths[taker]) // 2
    slack = jnp.where((donor == order[0]) | (taker == order[0]) | (lengths[taker] == 0), 0, jnp.maximum(slack, 0))
    moved = jax.random.randint(jax.random.fold_in(own, 4), (amount // 2,), 0, 1 << 20) % (slack + 1)
    lengths = lengths.at[donor].add(-moved).at[taker].add(moved)
    members = jnp.searchsorted(jnp.cumsum(lengths), jnp.arange(rows * top), side="right").astype(jnp.int32)
    grid = members.reshape(top, rows).T
    grid = grid[jax.random.permutation(jax.random.fold_in(own, 1), rows)]
    turn = jax.random.randint(jax.random.fold_in(own, 2), (rows, 1), 0, top)
    return jnp.take_along_axis(grid, (jnp.arange(top)[None, :] + turn) % top, axis=1)


def shares(count, total, bound, slope, full):
    portions = [(1 << 20) // math.isqrt(standing ** slope) + 1 for standing in range(1, count + 1)]
    largest = bound if full else min(bound, max(-(-total // count), total * portions[0] // sum(portions)))
    least = 1 if total - largest >= count - 1 else 0
    holding, rest = [largest] + [least] * (count - 1), total - largest - least * (count - 1)
    while rest > 0:
        free = [i for i in range(1, count) if holding[i] < largest] or [i for i in range(1, count) if holding[i] < bound]
        pool, budget = sum([portions[i] for i in free]), rest
        for i in free:
            more = min(bound - holding[i], max(1, budget * portions[i] // pool), rest)
            holding[i] = holding[i] + more
            rest = rest - more
    return np.array(holding)


def centred(rng, dims, scale, bound, split=(), held_as=jnp.bfloat16):
    level = block_scale(rng, dims, split, -0.22, 0.18) if split else 1.0
    array = jax.random.normal(rng, dims, jnp.float32) * scale * level
    return jnp.minimum(jnp.maximum(array, -bound), bound).astype(held_as)


def setup_inputs(seed: int = 0) -> dict:
    streams_of = jax.random.split(jax.random.key(seed), 9)
    tokens = centred(streams_of[0], (TOKENS, D), 1.0, 6.0, ((0, 32),))
    cotangent = centred(streams_of[1], (TOKENS, D), D ** -0.5, 0.09375, ((0, 32),))
    expert_ids_keys = jax.random.split(jax.random.fold_in(streams_of[2], 1), TOKENS // TOK_DEV)
    expert_ids_turns = jax.random.permutation(jax.random.fold_in(streams_of[2], 3), TOKENS // TOK_DEV)
    expert_ids = jax.vmap(lambda own, number: assign_block(jax.random.fold_in(streams_of[2], 2), own, number, TOK_DEV, ALL_EXPERTS, TOPK, CAP, 2))(expert_ids_keys, expert_ids_turns).reshape((TOKENS, TOPK))
    gates = jnp.clip(jnp.exp(math.log(1.0) - 2.9996462 * jax.random.uniform(streams_of[3], (TOKENS, TOPK), jnp.float32) ** block_scale(streams_of[3], (TOKENS, TOPK), ((0, 32),), -0.2, 0.2)), 0.049804688, 1.0).astype(jnp.bfloat16)
    swap_flags = with_ends((jax.random.randint(streams_of[4], (HALF,), 0, 2) < 1).astype(jnp.int32), jax.random.fold_in(streams_of[4], 1), 0, 1)
    gate_w = centred(streams_of[5], (EXPERTS, D, F), D ** -0.5, 0.09375, ((0, 16), (2, 2)))
    up_w = centred(streams_of[6], (EXPERTS, D, F), D ** -0.5, 0.09375, ((0, 16), (2, 2)))
    down_w = centred(streams_of[7], (EXPERTS, F, D), F ** -0.5, 0.1875, ((0, 16), (1, 2)))
    return {"tokens": tokens, "cotangent": cotangent, "expert_ids": expert_ids, "gates": gates, "swap_flags": swap_flags, "gate_w": gate_w, "up_w": up_w, "down_w": down_w}


def reference(tokens, cotangent, expert_ids, gates, swap_flags, gate_w, up_w, down_w):
    most_rows = CAP * N_DP * N_EXPERT
    flat_ids = expert_ids.reshape(-1).astype(jnp.int32)
    choice_count = flat_ids.shape[0]
    valid = flat_ids < EXPERTS
    sort_keys = jnp.where(valid, flat_ids, EXPERTS).astype(jnp.int32)
    order = jnp.argsort(sort_keys, stable=True).astype(jnp.int32)
    counts = jnp.sum(jnp.where(sort_keys[:, None] == jnp.arange(EXPERTS, dtype=jnp.int32)[None, :], 1, 0), axis=0).astype(jnp.int32)
    starts = (jnp.cumsum(counts) - counts).astype(jnp.int32)
    order_pad = jnp.concatenate([order, jnp.zeros((most_rows,), jnp.int32)])
    flat_gates = gates.reshape(-1)
    contract = (((0,), (0,)), ((), ()))

    def one_expert(expert):
        index = lax.dynamic_slice_in_dim(order_pad, starts[expert], most_rows)
        live = jnp.arange(most_rows, dtype=jnp.int32) < counts[expert]
        token_index = (index // TOPK).astype(jnp.int32)
        row_x = jnp.where(live[:, None], tokens[token_index], jnp.zeros((), tokens.dtype))
        row_dy = jnp.where(live[:, None], cotangent[token_index], jnp.zeros((), cotangent.dtype))
        row_g = jnp.where(live, flat_gates[index], jnp.zeros((), gates.dtype)).reshape(-1, 1)
        w_gate = gate_w[expert]
        w_up = up_w[expert]
        w_down = down_w[expert]
        pre_gate = jnp.dot(row_x, w_gate, preferred_element_type=jnp.float32)
        pre_up = jnp.dot(row_x, w_up, preferred_element_type=jnp.float32)
        sigma = jax.nn.sigmoid(pre_gate)
        active = pre_gate * sigma
        hidden = (active * pre_up).astype(jnp.bfloat16)
        back = lax.dot_general(row_dy, w_down, (((1,), (1,)), ((), ())), preferred_element_type=jnp.float32)
        score = jnp.sum(hidden.astype(jnp.float32) * back, axis=1)
        scaled = row_dy * row_g
        d_hidden = row_g.astype(jnp.float32) * back
        d_gate = (d_hidden * pre_up * sigma * (1.0 + pre_gate * (1.0 - sigma))).astype(jnp.bfloat16)
        d_up = (d_hidden * active).astype(jnp.bfloat16)
        grad_gate = lax.dot_general(row_x, d_gate, contract, preferred_element_type=jnp.float32)
        grad_up = lax.dot_general(row_x, d_up, contract, preferred_element_type=jnp.float32)
        grad_down = lax.dot_general(hidden, scaled, contract, preferred_element_type=jnp.float32)
        places = jnp.where(live, index, choice_count).astype(jnp.int32)
        return (grad_gate.astype(jnp.bfloat16), grad_up.astype(jnp.bfloat16), grad_down.astype(jnp.bfloat16), score, places)

    grads_gate, grads_up, grads_down, scores, places = lax.map(one_expert, jnp.arange(EXPERTS, dtype=jnp.int32))
    score_flat = jnp.zeros((choice_count + 1,), jnp.float32).at[places.reshape(-1)].set(scores.reshape(-1).astype(jnp.float32))
    score_grad = score_flat[:choice_count].reshape(expert_ids.shape)
    slot_ids = jnp.arange(EXPERTS, dtype=jnp.int32)
    holder = jnp.where(swap_flags[slot_ids % HALF] == 1, jnp.bitwise_xor(slot_ids, HALF), slot_ids).astype(jnp.int32)
    return (grads_gate[holder], grads_up[holder], grads_down[holder], score_grad)
```

```python
import functools
import math

import jax
import jax.numpy as jnp
from jax import lax
from jax.experimental import pallas as pl
from jax.experimental.pallas import tpu as pltpu
from jax.sharding import PartitionSpec as P

CAP = 6
CUTS = 4
SUB = CAP * CUTS
BLOCK = 2 * SUB
LANES = 128
AHEAD = 2
MIB = 1024 * 1024


def params(*arrays):
    held = sum(math.prod(shape) * size for shape, size in arrays)
    return pltpu.CompilerParams(vmem_limit_bytes=min(56 * MIB, held + 6 * MIB))


def pack_kernel(half, place_ref, ids_ref, gates_ref, tokens_ref, cot_ref, *refs):
    wire0_ref, wire1_ref, mine_ref, theirs_ref, pos_ref, rows_ref, sems = refs
    top, count = ids_ref.shape
    quarter = tokens_ref.shape[1] // CUTS
    experts = 2 * half
    copies = []
    for kind, source in enumerate((tokens_ref, cot_ref)):
        for q in range(CUTS):
            n = kind * CUTS + q
            copies.append(
                pltpu.make_async_copy(
                    source.at[:, pl.ds(q * quarter, quarter)],
                    rows_ref.at[pl.ds(n * count, count), :],
                    sems.at[n],
                )
            )
            copies[-1].start()
    ids = ids_ref[...]
    gates = gates_ref[...].astype(jnp.float32)
    expert = lax.broadcasted_iota(jnp.int32, (experts, count), 0)
    named = jnp.zeros((experts, count), jnp.float32)
    gate_of = jnp.zeros((experts, count), jnp.float32)
    for k in range(top):
        hit = ids[k : k + 1, :] == expert
        named = named + jnp.where(hit, 1.0, 0.0)
        gate_of = gate_of + jnp.where(hit, gates[k : k + 1, :], 0.0)
    earlier = lax.broadcasted_iota(jnp.int32, (count, count), 0) < lax.broadcasted_iota(
        jnp.int32, (count, count), 1
    )
    rank = jnp.dot(
        named.astype(jnp.bfloat16),
        jnp.where(earlier, 1.0, 0.0).astype(jnp.bfloat16),
        preferred_element_type=jnp.float32,
    )
    place = (expert * CAP + 1).astype(jnp.float32) + rank
    line = lax.broadcasted_iota(jnp.int32, (top, count), 0)
    pos = jnp.zeros((top, count), jnp.float32)
    for k in range(top):
        found = jnp.sum(jnp.where(ids[k : k + 1, :] == expert, place, 0.0), axis=0, keepdims=True)
        pos = jnp.where(line == k, found, pos)
    pos_ref[...] = pos.astype(jnp.int32) - 1
    per_token = jnp.concatenate([named, rank, gate_of], axis=1).astype(jnp.bfloat16)
    rows = half * BLOCK
    sub = lax.broadcasted_iota(jnp.int32, (rows, 1), 0)
    kind_cut = (sub % BLOCK) // CAP
    nth = (sub % CAP).astype(jnp.float32)
    low, side = place_ref[0] % half, place_ref[0] // half
    owner = lax.broadcasted_iota(jnp.int32, (rows, experts), 1)
    for rel, wire_ref in ((0, wire0_ref), (1, wire1_ref)):
        wanted = sub // BLOCK + half * (1 - side if rel else side)
        spread = jnp.where(owner == wanted, 1.0, 0.0).astype(jnp.bfloat16)
        seen = jnp.dot(spread, per_token, preferred_element_type=jnp.float32)
        chosen = (seen[:, :count] > 0.5) & (seen[:, count : 2 * count] == nth)
        pick_x = jnp.where(chosen, 1.0, 0.0)
        pick_s = jnp.where(chosen, seen[:, 2 * count :], 0.0)
        picks = [jnp.where(kind_cut == q, pick_x, 0.0) for q in range(CUTS)]
        picks += [jnp.where(kind_cut == CUTS + q, pick_s, 0.0) for q in range(CUTS)]
        picks = jnp.concatenate(picks, axis=1).astype(jnp.bfloat16)
        if rel == 0:
            for copy in copies:
                copy.wait()
        wire_ref[...] = jnp.dot(
            picks, rows_ref[...], preferred_element_type=jnp.float32
        ).astype(jnp.bfloat16)
    for core, turned_ref in enumerate((mine_ref, theirs_ref)):
        for c in range(half // 2):
            source = pl.multiple_of(jnp.bitwise_xor(low, 2 * c + core) * BLOCK, BLOCK)
            turned_ref[c * BLOCK : (c + 1) * BLOCK, :] = wire1_ref[pl.ds(source, BLOCK), :]


def pack(place, ids, gates, tokens, cotangent, half):
    count, width = tokens.shape
    quarter = width // CUTS
    vmem = pl.BlockSpec(memory_space=pltpu.VMEM)
    hbm = pl.BlockSpec(memory_space=pltpu.HBM)
    wire = jax.ShapeDtypeStruct((half * BLOCK, quarter), jnp.bfloat16)
    halved = jax.ShapeDtypeStruct((half * BLOCK // 2, quarter), jnp.bfloat16)
    return pl.pallas_call(
        functools.partial(pack_kernel, half),
        out_shape=(wire, wire, halved, halved, jax.ShapeDtypeStruct(ids.shape, jnp.int32)),
        in_specs=[pl.BlockSpec(memory_space=pltpu.SMEM), vmem, vmem, hbm, hbm],
        out_specs=(vmem,) * 5,
        scratch_shapes=[
            pltpu.VMEM((2 * CUTS * count, quarter), jnp.bfloat16),
            pltpu.SemaphoreType.DMA((2 * CUTS,)),
        ],
        compiler_params=pltpu.CompilerParams(vmem_limit_bytes=56 * MIB),
        name="pack",
    )(place, ids, gates, tokens, cotangent)


def order_matrix(half, turn):
    rows = half * BLOCK
    out = lax.broadcasted_iota(jnp.int32, (rows, 1), 0)
    sub = lax.broadcasted_iota(jnp.int32, (rows, rows), 1)
    group, inner = out // (half * CAP), out % (half * CAP)
    wanted = jnp.bitwise_xor(inner // CAP, turn) * BLOCK + group * CAP + inner % CAP
    return jnp.where(wanted == sub, 1.0, 0.0).astype(jnp.bfloat16)


def home_kernel(half, wires, *refs):
    wire_refs = refs[:wires]
    sources = refs[wires : wires + 3]
    acts_ref, score_ref, x_ref, s_ref, gate_ref, up_ref, down_ref, sems = refs[wires + 3 :]
    rows = half * CAP
    quarter = wire_refs[0].shape[1]
    hidden_width = gate_ref.shape[1]
    copies = []
    for q in range(CUTS):
        columns = pl.ds(q * quarter, quarter)
        for n, (source, target) in enumerate(zip(sources, (gate_ref, up_ref, down_ref))):
            place = (slice(None), columns) if n == 2 else (columns, slice(None))
            copies.append(
                pltpu.make_async_copy(source.at[place], target.at[place], sems.at[3 * q + n])
            )
    for copy in copies[: 3 * AHEAD]:
        copy.start()
    order = order_matrix(half, 0)
    for w in range(wires):
        sorted_rows = jnp.dot(
            order, wire_refs[w][...], preferred_element_type=jnp.float32
        ).astype(jnp.bfloat16)
        for q in range(CUTS):
            place = (q, pl.ds(w * rows, rows))
            x_ref[place] = sorted_rows[q * rows : (q + 1) * rows]
            s_ref[place] = sorted_rows[(CUTS + q) * rows : (CUTS + q + 1) * rows]
    total = wires * rows
    pre_gate = pre_up = d_hidden = jnp.zeros((total, hidden_width), jnp.float32)
    for q in range(CUTS):
        columns = pl.ds(q * quarter, quarter)
        for copy in copies[3 * q : 3 * q + 3]:
            copy.wait()
        for copy in copies[3 * (q + AHEAD) : 3 * (q + AHEAD) + 3]:
            copy.start()
        pre_gate += jnp.dot(x_ref[q], gate_ref[columns, :], preferred_element_type=jnp.float32)
        pre_up += jnp.dot(x_ref[q], up_ref[columns, :], preferred_element_type=jnp.float32)
        d_hidden += lax.dot_general(
            s_ref[q],
            down_ref[:, columns],
            (((1,), (1,)), ((), ())),
            preferred_element_type=jnp.float32,
        )
    sigma = 1.0 / (1.0 + jnp.exp(-pre_gate))
    active = pre_gate * sigma
    hidden = (active * pre_up).astype(jnp.bfloat16)
    d_gate = d_hidden * pre_up * sigma * (1.0 + pre_gate * (1.0 - sigma))
    acts_ref[:, :hidden_width] = hidden
    acts_ref[:, hidden_width : 2 * hidden_width] = d_gate.astype(jnp.bfloat16)
    acts_ref[:, 2 * hidden_width :] = (d_hidden * active).astype(jnp.bfloat16)
    score = jnp.sum(hidden.astype(jnp.float32) * d_hidden, axis=1, keepdims=True)
    row = lax.broadcasted_iota(jnp.int32, (total, 1), 0) % CAP
    lane = lax.broadcasted_iota(jnp.int32, (total, LANES), 1)
    spread = jnp.where(row == lane, score, 0.0)
    line = lax.broadcasted_iota(jnp.int32, (wires * half, 1), 0)
    group = (line % wires) * rows + (line // wires) * CAP
    member = lax.broadcasted_iota(jnp.int32, (wires * half, total), 1)
    score_ref[...] = jnp.dot(
        jnp.where((member >= group) & (member < group + CAP), 1.0, 0.0),
        spread,
        precision=lax.Precision.HIGHEST,
        preferred_element_type=jnp.float32,
    )


def home(wires, w_gate, w_up, w_down, half):
    width, hidden_width = w_gate.shape
    count = len(wires)
    rows = count * half * CAP
    vmem = pl.BlockSpec(memory_space=pltpu.VMEM)
    hbm = pl.BlockSpec(memory_space=pltpu.HBM)
    scratch = pltpu.VMEM((CUTS, rows, width // CUTS), jnp.bfloat16)
    return pl.pallas_call(
        functools.partial(home_kernel, half, count),
        out_shape=(
            jax.ShapeDtypeStruct((rows, 3 * hidden_width), jnp.bfloat16),
            jax.ShapeDtypeStruct((count * half, LANES), jnp.float32),
        ),
        in_specs=[vmem] * count + [hbm] * 3,
        out_specs=(vmem, vmem),
        scratch_shapes=[scratch, scratch]
        + [pltpu.VMEM(w.shape, jnp.bfloat16) for w in (w_gate, w_up, w_down)]
        + [pltpu.SemaphoreType.DMA((3 * CUTS,))],
        compiler_params=pltpu.CompilerParams(vmem_limit_bytes=56 * MIB),
        name="home",
    )(*wires, w_gate, w_up, w_down)


def sort_kernel(half, wires, turns, slot_ref, flag_ref, *refs):
    own_wires, slot_wires = refs[:wires], refs[wires : 2 * wires]
    x_ref, s_ref, wire_ref, sems = refs[2 * wires :]
    rows = half * CAP
    taken = flag_ref[0] == 1

    def fetch(w, source):
        pltpu.make_async_copy(source, wire_ref.at[w], sems.at[w]).start()

    for w in range(wires):
        pl.when(taken)(functools.partial(fetch, w, slot_wires[w]))
        pl.when(jnp.logical_not(taken))(functools.partial(fetch, w, own_wires[w]))
    order = order_matrix(half, jnp.where(taken, slot_ref[0] % half, 0) if turns else 0)
    for w in range(wires):
        pltpu.make_async_copy(own_wires[w], wire_ref.at[w], sems.at[w]).wait()
        sorted_rows = jnp.dot(order, wire_ref[w], preferred_element_type=jnp.float32).astype(
            jnp.bfloat16
        )
        for q in range(CUTS):
            x_ref[q, pl.ds(w * rows, rows), :] = sorted_rows[q * rows : (q + 1) * rows]
            s_ref[q, pl.ds(w * rows, rows), :] = sorted_rows[
                (CUTS + q) * rows : (CUTS + q + 1) * rows
            ]


def sort_rows(slot, flag, own_wires, slot_wires, turns, half):
    count = len(own_wires)
    quarter = own_wires[0].shape[1]
    rows = count * half * CAP
    vmem = pl.BlockSpec(memory_space=pltpu.VMEM)
    hbm = pl.BlockSpec(memory_space=pltpu.HBM)
    smem = pl.BlockSpec(memory_space=pltpu.SMEM)
    shape = jax.ShapeDtypeStruct((CUTS, rows, quarter), jnp.bfloat16)
    return pl.pallas_call(
        functools.partial(sort_kernel, half, count, turns),
        out_shape=(shape, shape),
        in_specs=[smem, smem] + [hbm] * (2 * count),
        out_specs=(vmem, vmem),
        scratch_shapes=[
            pltpu.VMEM((count, half * BLOCK, quarter), jnp.bfloat16),
            pltpu.SemaphoreType.DMA((count,)),
        ],
        compiler_params=params(((rows, CUTS * quarter), 2 * 2), (own_wires[0].shape, 2 * count + 8)),
        name="sort_rows",
    )(slot, flag, *own_wires, *slot_wires)


def grads_kernel(parts, flag_ref, *refs):
    own_refs, other_refs = refs[:parts], refs[parts : 2 * parts]
    x_refs, s_refs = refs[2 * parts : 3 * parts], refs[3 * parts : 4 * parts]
    gate_ref, up_ref, down_ref, acts_ref = refs[4 * parts :]
    rows = own_refs[0].shape[0]
    hidden_width = gate_ref.shape[1]

    @pl.when(pl.program_id(0) == 0)
    def _():
        taken = flag_ref[0] == 1
        for p in range(parts):
            acts_ref[pl.ds(p * rows, rows), :] = jnp.where(
                taken, other_refs[p][...], own_refs[p][...]
            )

    contract = (((0,), (0,)), ((), ()))
    x = jnp.concatenate([ref[0] for ref in x_refs], axis=0)
    s = jnp.concatenate([ref[0] for ref in s_refs], axis=0)
    out = lax.dot_general(
        x, acts_ref[:, hidden_width:], contract, preferred_element_type=jnp.float32
    )
    gate_ref[...] = out[:, :hidden_width].astype(jnp.bfloat16)
    up_ref[...] = out[:, hidden_width:].astype(jnp.bfloat16)
    down_ref[...] = lax.dot_general(
        acts_ref[:, :hidden_width], s, contract, preferred_element_type=jnp.float32
    ).astype(jnp.bfloat16)


def grads(flag, own, other, x_parts, s_parts):
    count = len(own)
    cuts, rows, quarter = x_parts[0].shape
    width = cuts * quarter
    triple = own[0].shape[1]
    hidden_width = triple // 3
    vmem = pl.BlockSpec(memory_space=pltpu.VMEM)
    part = pl.BlockSpec((1, rows, quarter), lambda q: (q, 0, 0))
    return pl.pallas_call(
        functools.partial(grads_kernel, count),
        grid=(cuts,),
        out_shape=(
            jax.ShapeDtypeStruct((width, hidden_width), jnp.bfloat16),
            jax.ShapeDtypeStruct((width, hidden_width), jnp.bfloat16),
            jax.ShapeDtypeStruct((hidden_width, width), jnp.bfloat16),
        ),
        in_specs=[pl.BlockSpec(memory_space=pltpu.SMEM)] + [vmem] * (2 * count) + [part] * (2 * count),
        out_specs=(
            pl.BlockSpec((quarter, hidden_width), lambda q: (q, 0)),
            pl.BlockSpec((quarter, hidden_width), lambda q: (q, 0)),
            pl.BlockSpec((hidden_width, quarter), lambda q: (0, q)),
        ),
        scratch_shapes=[pltpu.VMEM((count * rows, triple), jnp.bfloat16)],
        compiler_params=params(
            ((count * rows, triple), 3 * 2),
            ((count * rows, quarter), 2 * 3 * 2),
            ((quarter, hidden_width), 3 * (2 * 2 + 4)),
        ),
        name="grads",
    )(flag, *own, *other, *x_parts, *s_parts)


def body(tokens, cotangent, expert_ids, gates, swap_flags, gate_w, up_w, down_w):
    axis_len = lax.axis_size("expert")
    planes = lax.axis_size("dp")
    half = axis_len // 2
    own_slot = lax.axis_index("expert")
    side, low = own_slot // half, own_slot % half
    quarter = tokens.shape[1] // CUTS
    groups = [list(range(half)), list(range(half, axis_len))]
    slot = own_slot.reshape(1)
    flag = lax.dynamic_slice_in_dim(swap_flags, low, 1, 0)

    def exchange(wire, name):
        with jax.named_scope("t_" + name):
            blocks = wire.reshape(half, BLOCK, quarter)
            moved = lax.all_to_all(
                blocks, "expert", split_axis=0, concat_axis=0, tiled=True, axis_index_groups=groups
            )
            return moved.reshape(half * BLOCK, quarter)

    def flip(block, by, name):
        with jax.named_scope("t_" + name):
            return lax.ppermute(block, "expert", [(i, i ^ by) for i in range(axis_len)])

    def across(block, name):
        return flip(block, half, name)

    def turned_exchange(mine, theirs, name, behind):
        pieces = []
        for c in range(half // 2):
            part = slice(c * BLOCK, (c + 1) * BLOCK)
            piece = jnp.concatenate([mine[part], theirs[part]], axis=0)
            pieces.append(flip(piece, 2 * c, name + str(c)) if c else piece)
        pieces = lax.optimization_barrier(tuple(pieces) + behind)[: half // 2]
        return jnp.concatenate(pieces, axis=0)

    def all_planes(wire, name):
        with jax.named_scope("t_" + name):
            return [wire] + [
                lax.ppermute(wire, "dp", [(i, (i + by) % planes) for i in range(planes)])
                for by in range(1, planes)
            ]

    def after(value, *others):
        return lax.optimization_barrier((value,) + others)[0]

    wire0, wire1, mine, theirs, pos = pack(
        slot, expert_ids.T, gates.T, tokens, cotangent, half
    )
    moved = across(wire1, "M")
    theirs = flip(theirs, 1, "A1c")
    home0 = exchange(wire0, "A0")
    homes0 = all_planes(home0, "xR0")
    slot1 = turned_exchange(mine, theirs, "A1", ())
    home1 = exchange(after(moved, slot1, *homes0[1:]), "A2")
    crossed = across(after(home0, moved, *homes0[1:]), "O")
    slots1 = all_planes(slot1, "xR1")
    homes1 = all_planes(home1, "xRM")
    homes1[0] = after(homes1[0], crossed, *slots1[1:])
    acts0, score0 = home(homes0, gate_w[0], up_w[0], down_w[0], half)
    slots0 = all_planes(after(crossed, acts0), "xO")
    acts1, score1 = home(homes1, gate_w[0], up_w[0], down_w[0], half)
    own = [acts0, acts1]
    other = [across(after(acts0, crossed), "acts0"), across(acts1, "acts1")]
    rows0 = sort_rows(slot, flag, homes0, slots0, False, half)
    rows1 = sort_rows(slot, flag, homes1, slots1, True, half)

    near = score0.reshape(half, planes, LANES)
    far = score1.reshape(half, planes, LANES)
    near, far = lax.optimization_barrier((near, far) + ())[:2]
    back = jnp.concatenate([jnp.where(side == 0, near, far), jnp.where(side == 0, far, near)])
    returned = lax.all_to_all(back, "expert", split_axis=0, concat_axis=0, tiled=True)
    returned = after(returned, rows0[0], rows1[0])
    sums = [returned[:, 0]]
    for by in range(1, planes):
        sums.append(
            lax.ppermute(returned[:, by], "dp", [(i, (i - by) % planes) for i in range(planes)])
        )

    out_gate, out_up, out_down = grads(
        flag, own, other, [rows0[0], rows1[0]], [rows0[1], rows1[1]]
    )
    total = sum(lax.optimization_barrier((*sums, out_down))[:-1])
    values = total[:, :CAP].reshape(-1)
    match = pos[:, :, None] == jnp.arange(axis_len * CAP, dtype=jnp.int32)[None, None, :]
    picked = jnp.sum(jnp.where(match, values[None, None, :], 0.0), axis=2)
    score_grad = (picked / gates.T.astype(jnp.float32)).T

    return (out_gate[None], out_up[None], out_down[None], score_grad)


def solution(mesh):
    placed = (
        P(("dp", "expert"), None),
        P(("dp", "expert"), None),
        P(("dp", "expert"), None),
        P(("dp", "expert"), None),
        P(),
        P("expert", None, "dp"),
        P("expert", None, "dp"),
        P("expert", "dp", None),
    )
    return jax.shard_map(
        body,
        mesh=mesh,
        in_specs=placed,
        out_specs=(
            P("expert", None, "dp"),
            P("expert", None, "dp"),
            P("expert", "dp", None),
            P(("dp", "expert"), None),
        ),
        check_vma=False,
    )
```

```python
import functools
import math

import jax
import jax.numpy as jnp
from jax import lax
from jax.experimental import pallas as pl
from jax.experimental.pallas import tpu as pltpu
from jax.sharding import PartitionSpec as P

CAP = 6
CUTS = 4
SUB = CAP * CUTS
BLOCK = 2 * SUB
LANES = 128
AHEAD = 2
MIB = 1024 * 1024


def params(*arrays):
    held = sum(math.prod(shape) * size for shape, size in arrays)
    return pltpu.CompilerParams(vmem_limit_bytes=min(56 * MIB, held + 6 * MIB))


def pack_kernel(half, place_ref, ids_ref, gates_ref, tokens_ref, cot_ref, *refs):
    wire0_ref, wire1_ref, mine_ref, theirs_ref, pos_ref, rows_ref, sems = refs
    top, count = ids_ref.shape
    quarter = tokens_ref.shape[1] // CUTS
    experts = 2 * half
    copies = []
    for kind, source in enumerate((tokens_ref, cot_ref)):
        for q in range(CUTS):
            n = kind * CUTS + q
            copies.append(
                pltpu.make_async_copy(
                    source.at[:, pl.ds(q * quarter, quarter)],
                    rows_ref.at[pl.ds(n * count, count), :],
                    sems.at[n],
                )
            )
            copies[-1].start()
    ids = ids_ref[...]
    gates = gates_ref[...].astype(jnp.float32)
    expert = lax.broadcasted_iota(jnp.int32, (experts, count), 0)
    named = jnp.zeros((experts, count), jnp.float32)
    gate_of = jnp.zeros((experts, count), jnp.float32)
    for k in range(top):
        hit = ids[k : k + 1, :] == expert
        named = named + jnp.where(hit, 1.0, 0.0)
        gate_of = gate_of + jnp.where(hit, gates[k : k + 1, :], 0.0)
    earlier = lax.broadcasted_iota(jnp.int32, (count, count), 0) < lax.broadcasted_iota(
        jnp.int32, (count, count), 1
    )
    rank = jnp.dot(
        named.astype(jnp.bfloat16),
        jnp.where(earlier, 1.0, 0.0).astype(jnp.bfloat16),
        preferred_element_type=jnp.float32,
    )
    place = (expert * CAP + 1).astype(jnp.float32) + rank
    line = lax.broadcasted_iota(jnp.int32, (top, count), 0)
    pos = jnp.zeros((top, count), jnp.float32)
    for k in range(top):
        found = jnp.sum(jnp.where(ids[k : k + 1, :] == expert, place, 0.0), axis=0, keepdims=True)
        pos = jnp.where(line == k, found, pos)
    pos_ref[...] = pos.astype(jnp.int32) - 1
    per_token = jnp.concatenate([named, rank, gate_of], axis=1).astype(jnp.bfloat16)
    rows = half * BLOCK
    sub = lax.broadcasted_iota(jnp.int32, (rows, 1), 0)
    kind_cut = (sub % BLOCK) // CAP
    nth = (sub % CAP).astype(jnp.float32)
    low, side = place_ref[0] % half, place_ref[0] // half
    owner = lax.broadcasted_iota(jnp.int32, (rows, experts), 1)
    for rel, wire_ref in ((0, wire0_ref), (1, wire1_ref)):
        wanted = sub // BLOCK + half * (1 - side if rel else side)
        spread = jnp.where(owner == wanted, 1.0, 0.0).astype(jnp.bfloat16)
        seen = jnp.dot(spread, per_token, preferred_element_type=jnp.float32)
        chosen = (seen[:, :count] > 0.5) & (seen[:, count : 2 * count] == nth)
        pick_x = jnp.where(chosen, 1.0, 0.0)
        pick_s = jnp.where(chosen, seen[:, 2 * count :], 0.0)
        picks = [jnp.where(kind_cut == q, pick_x, 0.0) for q in range(CUTS)]
        picks += [jnp.where(kind_cut == CUTS + q, pick_s, 0.0) for q in range(CUTS)]
        picks = jnp.concatenate(picks, axis=1).astype(jnp.bfloat16)
        if rel == 0:
            for copy in copies:
                copy.wait()
        wire_ref[...] = jnp.dot(
            picks, rows_ref[...], preferred_element_type=jnp.float32
        ).astype(jnp.bfloat16)
    for core, turned_ref in enumerate((mine_ref, theirs_ref)):
        for c in range(half // 2):
            source = pl.multiple_of(jnp.bitwise_xor(low, 2 * c + core) * BLOCK, BLOCK)
            turned_ref[c * BLOCK : (c + 1) * BLOCK, :] = wire1_ref[pl.ds(source, BLOCK), :]


def pack(place, ids, gates, tokens, cotangent, half):
    count, width = tokens.shape
    quarter = width // CUTS
    vmem = pl.BlockSpec(memory_space=pltpu.VMEM)
    hbm = pl.BlockSpec(memory_space=pltpu.HBM)
    wire = jax.ShapeDtypeStruct((half * BLOCK, quarter), jnp.bfloat16)
    halved = jax.ShapeDtypeStruct((half * BLOCK // 2, quarter), jnp.bfloat16)
    return pl.pallas_call(
        functools.partial(pack_kernel, half),
        out_shape=(wire, wire, halved, halved, jax.ShapeDtypeStruct(ids.shape, jnp.int32)),
        in_specs=[pl.BlockSpec(memory_space=pltpu.SMEM), vmem, vmem, hbm, hbm],
        out_specs=(vmem,) * 5,
        scratch_shapes=[
            pltpu.VMEM((2 * CUTS * count, quarter), jnp.bfloat16),
            pltpu.SemaphoreType.DMA((2 * CUTS,)),
        ],
        compiler_params=pltpu.CompilerParams(vmem_limit_bytes=56 * MIB),
        name="pack",
    )(place, ids, gates, tokens, cotangent)


def order_matrix(half, turn):
    rows = half * BLOCK
    out = lax.broadcasted_iota(jnp.int32, (rows, 1), 0)
    sub = lax.broadcasted_iota(jnp.int32, (rows, rows), 1)
    group, inner = out // (half * CAP), out % (half * CAP)
    wanted = jnp.bitwise_xor(inner // CAP, turn) * BLOCK + group * CAP + inner % CAP
    return jnp.where(wanted == sub, 1.0, 0.0).astype(jnp.bfloat16)


def home_kernel(half, wires, last, *refs):
    if last:
        slot_ref, plane_ref, flags_ref, near_ref, *refs = refs
        slot_wires, refs = refs[:wires], refs[wires:]
    wire_refs = refs[:wires]
    sources = refs[wires : wires + 3]
    acts_ref, score_ref, *refs = refs[wires + 3 :]
    if last:
        picked_x_ref, picked_s_ref, *refs = refs
        picked_ref, *refs = refs
    x_ref, s_ref, gate_ref, up_ref, down_ref, sems = refs
    rows = half * CAP
    quarter = wire_refs[0].shape[1]
    hidden_width = gate_ref.shape[1]
    copies = []
    for q in range(CUTS):
        columns = pl.ds(q * quarter, quarter)
        for n, (source, target) in enumerate(zip(sources, (gate_ref, up_ref, down_ref))):
            place = (slice(None), columns) if n == 2 else (columns, slice(None))
            copies.append(
                pltpu.make_async_copy(source.at[place], target.at[place], sems.at[3 * q + n])
            )
    if last:
        low, side = slot_ref[0] % half, slot_ref[0] // half
        taken = flags_ref[low] == 1
        for w in range(wires):
            fetch = pltpu.make_async_copy(slot_wires[w], picked_ref.at[w], sems.at[3 * CUTS + w])
            pl.when(taken)(fetch.start)
    for copy in copies[: 3 * AHEAD]:
        copy.start()
    order = order_matrix(half, 0)
    for w in range(wires):
        sorted_rows = jnp.dot(
            order, wire_refs[w][...], preferred_element_type=jnp.float32
        ).astype(jnp.bfloat16)
        for q in range(CUTS):
            place = (q, pl.ds(w * rows, rows))
            x_ref[place] = sorted_rows[q * rows : (q + 1) * rows]
            s_ref[place] = sorted_rows[(CUTS + q) * rows : (CUTS + q + 1) * rows]
    if last:

        @pl.when(taken)
        def _():
            turned = order_matrix(half, low)
            for w in range(wires):
                pltpu.make_async_copy(
                    slot_wires[w], picked_ref.at[w], sems.at[3 * CUTS + w]
                ).wait()
                picked = jnp.dot(
                    turned, picked_ref[w], preferred_element_type=jnp.float32
                ).astype(jnp.bfloat16)
                for q in range(CUTS):
                    place = (q, pl.ds(w * rows, rows))
                    picked_x_ref[place] = picked[q * rows : (q + 1) * rows]
                    picked_s_ref[place] = picked[(CUTS + q) * rows : (CUTS + q + 1) * rows]

        @pl.when(jnp.logical_not(taken))
        def _():
            picked_x_ref[...] = x_ref[...]
            picked_s_ref[...] = s_ref[...]

    total = wires * rows
    pre_gate = pre_up = d_hidden = jnp.zeros((total, hidden_width), jnp.float32)
    for q in range(CUTS):
        columns = pl.ds(q * quarter, quarter)
        for copy in copies[3 * q : 3 * q + 3]:
            copy.wait()
        for copy in copies[3 * (q + AHEAD) : 3 * (q + AHEAD) + 3]:
            copy.start()
        pre_gate += jnp.dot(x_ref[q], gate_ref[columns, :], preferred_element_type=jnp.float32)
        pre_up += jnp.dot(x_ref[q], up_ref[columns, :], preferred_element_type=jnp.float32)
        d_hidden += lax.dot_general(
            s_ref[q],
            down_ref[:, columns],
            (((1,), (1,)), ((), ())),
            preferred_element_type=jnp.float32,
        )
    sigma = 1.0 / (1.0 + jnp.exp(-pre_gate))
    active = pre_gate * sigma
    hidden = (active * pre_up).astype(jnp.bfloat16)
    d_gate = d_hidden * pre_up * sigma * (1.0 + pre_gate * (1.0 - sigma))
    acts_ref[:, :hidden_width] = hidden
    acts_ref[:, hidden_width : 2 * hidden_width] = d_gate.astype(jnp.bfloat16)
    acts_ref[:, 2 * hidden_width :] = (d_hidden * active).astype(jnp.bfloat16)
    score = jnp.sum(hidden.astype(jnp.float32) * d_hidden, axis=1, keepdims=True)
    row = lax.broadcasted_iota(jnp.int32, (total, 1), 0) % CAP
    lane = lax.broadcasted_iota(jnp.int32, (total, LANES), 1)
    spread = jnp.where(row == lane, score, 0.0)
    line = lax.broadcasted_iota(jnp.int32, (wires * half, 1), 0)
    group = (line // half) * rows + (line % half) * CAP
    member = lax.broadcasted_iota(jnp.int32, (wires * half, total), 1)
    scores = jnp.dot(
        jnp.where((member >= group) & (member < group + CAP), 1.0, 0.0),
        spread,
        precision=lax.Precision.HIGHEST,
        preferred_element_type=jnp.float32,
    )
    if last:
        for w in range(wires):
            part = slice(w * half, (w + 1) * half)
            first = 2 * half * ((plane_ref[0] - w + wires) % wires)
            near_rows = pl.ds(pl.multiple_of(first + half * side, half), half)
            far_rows = pl.ds(pl.multiple_of(first + half * (1 - side), half), half)
            score_ref[near_rows, :] = near_ref[part, :]
            score_ref[far_rows, :] = scores[part]
    else:
        score_ref[...] = scores


def home(wires, weights, half, *more):
    width, hidden_width = weights[0].shape
    count = len(wires)
    rows = count * half * CAP
    vmem = pl.BlockSpec(memory_space=pltpu.VMEM)
    hbm = pl.BlockSpec(memory_space=pltpu.HBM)
    smem = pl.BlockSpec(memory_space=pltpu.SMEM)
    parts = (CUTS, rows, width // CUTS)
    scratch = pltpu.VMEM(parts, jnp.bfloat16)
    out_shape = [
        jax.ShapeDtypeStruct((rows, 3 * hidden_width), jnp.bfloat16),
        jax.ShapeDtypeStruct((count * half * (2 if more else 1), LANES), jnp.float32),
    ]
    if more:
        out_shape += [jax.ShapeDtypeStruct(parts, jnp.bfloat16)] * 2
    return pl.pallas_call(
        functools.partial(home_kernel, half, count, bool(more)),
        out_shape=out_shape,
        in_specs=([smem, smem, smem, vmem] + [hbm] * count if more else []) + [vmem] * count + [hbm] * 3,
        out_specs=[vmem] * len(out_shape),
        scratch_shapes=([pltpu.VMEM((count,) + wires[0].shape, jnp.bfloat16)] if more else [])
        + [scratch, scratch]
        + [pltpu.VMEM(w.shape, jnp.bfloat16) for w in weights]
        + [pltpu.SemaphoreType.DMA((3 * CUTS + count,))],
        compiler_params=pltpu.CompilerParams(vmem_limit_bytes=56 * MIB),
        name="home_last" if more else "home",
    )(*more, *wires, *weights)


def sort_kernel(half, wires, slot_ref, flags_ref, *refs):
    own_wires, slot_wires = refs[:wires], refs[wires : 2 * wires]
    x_ref, s_ref, wire_ref, sems = refs[2 * wires :]
    rows = half * CAP
    taken = flags_ref[slot_ref[0] % half] == 1

    def fetch(w, source):
        pltpu.make_async_copy(source, wire_ref.at[w], sems.at[w]).start()

    for w in range(wires):
        pl.when(taken)(functools.partial(fetch, w, slot_wires[w]))
        pl.when(jnp.logical_not(taken))(functools.partial(fetch, w, own_wires[w]))
    order = order_matrix(half, 0)
    for w in range(wires):
        pltpu.make_async_copy(own_wires[w], wire_ref.at[w], sems.at[w]).wait()
        sorted_rows = jnp.dot(order, wire_ref[w], preferred_element_type=jnp.float32).astype(
            jnp.bfloat16
        )
        for q in range(CUTS):
            x_ref[q, pl.ds(w * rows, rows), :] = sorted_rows[q * rows : (q + 1) * rows]
            s_ref[q, pl.ds(w * rows, rows), :] = sorted_rows[
                (CUTS + q) * rows : (CUTS + q + 1) * rows
            ]


def sort_rows(slot, flags, own_wires, slot_wires, half):
    count = len(own_wires)
    quarter = own_wires[0].shape[1]
    rows = count * half * CAP
    vmem = pl.BlockSpec(memory_space=pltpu.VMEM)
    hbm = pl.BlockSpec(memory_space=pltpu.HBM)
    smem = pl.BlockSpec(memory_space=pltpu.SMEM)
    shape = jax.ShapeDtypeStruct((CUTS, rows, quarter), jnp.bfloat16)
    return pl.pallas_call(
        functools.partial(sort_kernel, half, count),
        out_shape=(shape, shape),
        in_specs=[smem, smem] + [hbm] * (2 * count),
        out_specs=(vmem, vmem),
        scratch_shapes=[
            pltpu.VMEM((count, half * BLOCK, quarter), jnp.bfloat16),
            pltpu.SemaphoreType.DMA((count,)),
        ],
        compiler_params=pltpu.CompilerParams(vmem_limit_bytes=56 * MIB),
        name="sort_rows",
    )(slot, flags, *own_wires, *slot_wires)


def grads_kernel(half, parts, slot_ref, flags_ref, *refs):
    own_refs, other_refs = refs[:parts], refs[parts : 2 * parts]
    x_refs, s_refs = refs[2 * parts : 3 * parts], refs[3 * parts : 4 * parts]
    gate_ref, up_ref, down_ref, acts_ref, sems = refs[4 * parts :]
    rows = own_refs[0].shape[0]
    hidden_width = gate_ref.shape[1]

    @pl.when(pl.program_id(0) == 0)
    def _():
        taken = flags_ref[slot_ref[0] % half] == 1
        for p in range(parts):
            target = acts_ref.at[pl.ds(p * rows, rows), :]
            pl.when(taken)(pltpu.make_async_copy(other_refs[p], target, sems.at[p]).start)
            pl.when(jnp.logical_not(taken))(
                pltpu.make_async_copy(own_refs[p], target, sems.at[p]).start
            )
        for p in range(parts):
            target = acts_ref.at[pl.ds(p * rows, rows), :]
            pltpu.make_async_copy(own_refs[p], target, sems.at[p]).wait()

    contract = (((0,), (0,)), ((), ()))
    x = jnp.concatenate([ref[0] for ref in x_refs], axis=0)
    s = jnp.concatenate([ref[0] for ref in s_refs], axis=0)
    out = lax.dot_general(
        x, acts_ref[:, hidden_width:], contract, preferred_element_type=jnp.float32
    )
    gate_ref[...] = out[:, :hidden_width].astype(jnp.bfloat16)
    up_ref[...] = out[:, hidden_width:].astype(jnp.bfloat16)
    down_ref[...] = lax.dot_general(
        acts_ref[:, :hidden_width], s, contract, preferred_element_type=jnp.float32
    ).astype(jnp.bfloat16)


def grads(slot, flags, own, other, x_parts, s_parts, half):
    count = len(own)
    cuts, rows, quarter = x_parts[0].shape
    width = cuts * quarter
    triple = own[0].shape[1]
    hidden_width = triple // 3
    hbm = pl.BlockSpec(memory_space=pltpu.HBM)
    smem = pl.BlockSpec(memory_space=pltpu.SMEM)
    part = pl.BlockSpec((1, rows, quarter), lambda q: (q, 0, 0))
    return pl.pallas_call(
        functools.partial(grads_kernel, half, count),
        grid=(cuts,),
        out_shape=(
            jax.ShapeDtypeStruct((width, hidden_width), jnp.bfloat16),
            jax.ShapeDtypeStruct((width, hidden_width), jnp.bfloat16),
            jax.ShapeDtypeStruct((hidden_width, width), jnp.bfloat16),
        ),
        in_specs=[smem, smem] + [hbm] * (2 * count) + [part] * (2 * count),
        out_specs=(
            pl.BlockSpec((quarter, hidden_width), lambda q: (q, 0)),
            pl.BlockSpec((quarter, hidden_width), lambda q: (q, 0)),
            pl.BlockSpec((hidden_width, quarter), lambda q: (0, q)),
        ),
        scratch_shapes=[
            pltpu.VMEM((count * rows, triple), jnp.bfloat16),
            pltpu.SemaphoreType.DMA((count,)),
        ],
        compiler_params=pltpu.CompilerParams(vmem_limit_bytes=56 * MIB),
        name="grads",
    )(slot, flags, *own, *other, *x_parts, *s_parts)


def body(tokens, cotangent, expert_ids, gates, swap_flags, gate_w, up_w, down_w):
    axis_len = lax.axis_size("expert")
    planes = lax.axis_size("dp")
    half = axis_len // 2
    own_slot = lax.axis_index("expert")
    quarter = tokens.shape[1] // CUTS
    groups = [list(range(half)), list(range(half, axis_len))]
    slot = own_slot.reshape(1)
    plane = lax.axis_index("dp").reshape(1)

    def exchange(wire, name):
        with jax.named_scope(name):
            blocks = wire.reshape(half, BLOCK, quarter)
            moved = lax.all_to_all(
                blocks, "expert", split_axis=0, concat_axis=0, tiled=True, axis_index_groups=groups
            )
            return moved.reshape(half * BLOCK, quarter)

    def flip(block, by, name):
        with jax.named_scope(name):
            return lax.ppermute(block, "expert", [(i, i ^ by) for i in range(axis_len)])

    def across(block, name):
        return flip(block, half, name)

    def turned_exchange(mine, theirs, name, behind):
        pieces = []
        for c in range(half // 2):
            part = slice(c * BLOCK, (c + 1) * BLOCK)
            piece = jnp.concatenate([mine[part], theirs[part]], axis=0)
            pieces.append(flip(piece, 2 * c, name + str(c)) if c else piece)
        pieces = lax.optimization_barrier(tuple(pieces) + behind)[: half // 2]
        return jnp.concatenate(pieces, axis=0)

    def all_planes(wire, name):
        with jax.named_scope(name):
            return [wire] + [
                lax.ppermute(wire, "dp", [(i, (i + by) % planes) for i in range(planes)])
                for by in range(1, planes)
            ]

    def after(value, *others):
        return lax.optimization_barrier((value,) + others)[0]

    wire0, wire1, mine, theirs, pos = pack(
        slot, expert_ids.T, gates.T, tokens, cotangent, half
    )
    moved = across(wire1, "rows_across")
    theirs = flip(theirs, 1, "slot_rows_cores")
    home0 = exchange(wire0, "home_rows_half")
    homes0 = all_planes(home0, "home_rows_planes")
    slot1 = turned_exchange(mine, theirs, "slot_rows_chips", ())
    home1 = exchange(after(moved, slot1, *homes0[1:]), "crossed_rows_half")
    crossed = across(after(home0, slot1), "home_rows_across")
    slots1 = all_planes(slot1, "slot_rows_planes")
    homes1 = all_planes(home1, "crossed_rows_planes")
    homes1[0] = after(homes1[0], crossed, *slots1[1:])
    weights = (gate_w[0], up_w[0], down_w[0])
    acts0, score0 = home(homes0, weights, half)
    slots0 = all_planes(after(crossed, acts0), "slot_crossed_planes")
    acts1, back, x_rows1, s_rows1 = home(
        homes1, weights, half, slot, plane, swap_flags, score0, *slots1
    )
    own = [acts0, acts1]
    other = [across(after(acts0, crossed), "acts_near_across"), across(acts1, "acts_far_across")]
    x_rows0, s_rows0 = sort_rows(slot, swap_flags, homes0, slots0, half)

    returned = lax.all_to_all(
        back.reshape(planes * axis_len, 1, LANES),
        ("dp", "expert"),
        split_axis=0,
        concat_axis=0,
        tiled=True,
    )
    out_gate, out_up, out_down = grads(
        slot, swap_flags, own, other, [x_rows0, x_rows1], [s_rows0, s_rows1], half
    )
    returned = after(returned, out_down)
    total = jnp.sum(returned.reshape(planes, axis_len, LANES), axis=0)
    values = total[:, :CAP].reshape(-1)
    match = pos[:, :, None] == jnp.arange(axis_len * CAP, dtype=jnp.int32)[None, None, :]
    picked = jnp.sum(jnp.where(match, values[None, None, :], 0.0), axis=2)
    score_grad = (picked / gates.T.astype(jnp.float32)).T

    return (out_gate[None], out_up[None], out_down[None], score_grad)


def solution(mesh):
    placed = (
        P(("dp", "expert"), None),
        P(("dp", "expert"), None),
        P(("dp", "expert"), None),
        P(("dp", "expert"), None),
        P(),
        P("expert", None, "dp"),
        P("expert", None, "dp"),
        P("expert", "dp", None),
    )
    return jax.shard_map(
        body,
        mesh=mesh,
        in_specs=placed,
        out_specs=(
            P("expert", None, "dp"),
            P("expert", None, "dp"),
            P("expert", "dp", None),
            P(("dp", "expert"), None),
        ),
        check_vma=False,
    )
```

```python
import functools
import math

import jax
import jax.numpy as jnp
from jax import lax
from jax.experimental import pallas as pl
from jax.experimental.pallas import tpu as pltpu
from jax.sharding import PartitionSpec as P

CAP = 6
CUTS = 4
SUB = CAP * CUTS
BLOCK = 2 * SUB
LANES = 128
AHEAD = 2
MIB = 1024 * 1024


def params(*arrays):
    held = sum(math.prod(shape) * size for shape, size in arrays)
    return pltpu.CompilerParams(vmem_limit_bytes=min(56 * MIB, max(24 * MIB, 4 * held)))


def pack_kernel(half, place_ref, ids_ref, gates_ref, tokens_ref, cot_ref, *refs):
    wire0_ref, wire1_ref, mine_ref, theirs_ref, pos_ref, rows_ref, sems = refs
    top, count = ids_ref.shape
    quarter = tokens_ref.shape[1] // CUTS
    experts = 2 * half
    copies = []
    for kind, source in enumerate((tokens_ref, cot_ref)):
        for q in range(CUTS):
            n = kind * CUTS + q
            copies.append(
                pltpu.make_async_copy(
                    source.at[:, pl.ds(q * quarter, quarter)],
                    rows_ref.at[pl.ds(n * count, count), :],
                    sems.at[n],
                )
            )
            copies[-1].start()
    ids = ids_ref[...]
    gates = gates_ref[...].astype(jnp.float32)
    expert = lax.broadcasted_iota(jnp.int32, (experts, count), 0)
    named = jnp.zeros((experts, count), jnp.float32)
    gate_of = jnp.zeros((experts, count), jnp.float32)
    for k in range(top):
        hit = ids[k : k + 1, :] == expert
        named = named + jnp.where(hit, 1.0, 0.0)
        gate_of = gate_of + jnp.where(hit, gates[k : k + 1, :], 0.0)
    earlier = lax.broadcasted_iota(jnp.int32, (count, count), 0) < lax.broadcasted_iota(
        jnp.int32, (count, count), 1
    )
    rank = jnp.dot(
        named.astype(jnp.bfloat16),
        jnp.where(earlier, 1.0, 0.0).astype(jnp.bfloat16),
        preferred_element_type=jnp.float32,
    )
    place = (expert * CAP + 1).astype(jnp.float32) + rank
    line = lax.broadcasted_iota(jnp.int32, (top, count), 0)
    pos = jnp.zeros((top, count), jnp.float32)
    for k in range(top):
        found = jnp.sum(jnp.where(ids[k : k + 1, :] == expert, place, 0.0), axis=0, keepdims=True)
        pos = jnp.where(line == k, found, pos)
    pos_ref[...] = pos.astype(jnp.int32) - 1
    per_token = jnp.concatenate([named, rank, gate_of], axis=1).astype(jnp.bfloat16)
    rows = half * BLOCK
    sub = lax.broadcasted_iota(jnp.int32, (rows, 1), 0)
    kind_cut = (sub % BLOCK) // CAP
    nth = (sub % CAP).astype(jnp.float32)
    low, side = place_ref[0] % half, place_ref[0] // half
    owner = lax.broadcasted_iota(jnp.int32, (rows, experts), 1)
    for rel, wire_ref in ((0, wire0_ref), (1, wire1_ref)):
        wanted = sub // BLOCK + half * (1 - side if rel else side)
        spread = jnp.where(owner == wanted, 1.0, 0.0).astype(jnp.bfloat16)
        seen = jnp.dot(spread, per_token, preferred_element_type=jnp.float32)
        chosen = (seen[:, :count] > 0.5) & (seen[:, count : 2 * count] == nth)
        pick_x = jnp.where(chosen, 1.0, 0.0)
        pick_s = jnp.where(chosen, seen[:, 2 * count :], 0.0)
        picks = [jnp.where(kind_cut == q, pick_x, 0.0) for q in range(CUTS)]
        picks += [jnp.where(kind_cut == CUTS + q, pick_s, 0.0) for q in range(CUTS)]
        picks = jnp.concatenate(picks, axis=1).astype(jnp.bfloat16)
        if rel == 0:
            for copy in copies:
                copy.wait()
        wire_ref[...] = jnp.dot(
            picks, rows_ref[...], preferred_element_type=jnp.float32
        ).astype(jnp.bfloat16)
    for core, turned_ref in enumerate((mine_ref, theirs_ref)):
        for c in range(half // 2):
            source = pl.multiple_of(jnp.bitwise_xor(low, 2 * c + core) * BLOCK, BLOCK)
            turned_ref[c * BLOCK : (c + 1) * BLOCK, :] = wire1_ref[pl.ds(source, BLOCK), :]


def pack(place, ids, gates, tokens, cotangent, half):
    count, width = tokens.shape
    quarter = width // CUTS
    vmem = pl.BlockSpec(memory_space=pltpu.VMEM)
    hbm = pl.BlockSpec(memory_space=pltpu.HBM)
    wire = jax.ShapeDtypeStruct((half * BLOCK, quarter), jnp.bfloat16)
    halved = jax.ShapeDtypeStruct((half * BLOCK // 2, quarter), jnp.bfloat16)
    return pl.pallas_call(
        functools.partial(pack_kernel, half),
        out_shape=(wire, wire, halved, halved, jax.ShapeDtypeStruct(ids.shape, jnp.int32)),
        in_specs=[pl.BlockSpec(memory_space=pltpu.SMEM), vmem, vmem, hbm, hbm],
        out_specs=(vmem,) * 5,
        scratch_shapes=[
            pltpu.VMEM((2 * CUTS * count, quarter), jnp.bfloat16),
            pltpu.SemaphoreType.DMA((2 * CUTS,)),
        ],
        compiler_params=pltpu.CompilerParams(vmem_limit_bytes=56 * MIB),
        name="pack",
    )(place, ids, gates, tokens, cotangent)


def order_matrix(half, turn):
    rows = half * BLOCK
    out = lax.broadcasted_iota(jnp.int32, (rows, 1), 0)
    sub = lax.broadcasted_iota(jnp.int32, (rows, rows), 1)
    group, inner = out // (half * CAP), out % (half * CAP)
    wanted = jnp.bitwise_xor(inner // CAP, turn) * BLOCK + group * CAP + inner % CAP
    return jnp.where(wanted == sub, 1.0, 0.0).astype(jnp.bfloat16)


def home_kernel(half, wires, last, *refs):
    if last:
        slot_ref, plane_ref, flags_ref, near_ref, *refs = refs
        slot_wires, refs = refs[:wires], refs[wires:]
    wire_refs = refs[:wires]
    sources = refs[wires : wires + 3]
    acts_ref, score_ref, *refs = refs[wires + 3 :]
    if last:
        picked_x_ref, picked_s_ref, *refs = refs
        picked_ref, *refs = refs
    x_ref, s_ref, gate_ref, up_ref, down_ref, sems = refs
    rows = half * CAP
    quarter = wire_refs[0].shape[1]
    hidden_width = gate_ref.shape[1]
    copies = []
    for q in range(CUTS):
        columns = pl.ds(q * quarter, quarter)
        for n, (source, target) in enumerate(zip(sources, (gate_ref, up_ref, down_ref))):
            place = (slice(None), columns) if n == 2 else (columns, slice(None))
            copies.append(
                pltpu.make_async_copy(source.at[place], target.at[place], sems.at[3 * q + n])
            )
    if last:
        low, side = slot_ref[0] % half, slot_ref[0] // half
        taken = flags_ref[low] == 1
        for w in range(wires):
            fetch = pltpu.make_async_copy(slot_wires[w], picked_ref.at[w], sems.at[3 * CUTS + w])
            pl.when(taken)(fetch.start)
    for copy in copies[: 3 * AHEAD]:
        copy.start()
    order = order_matrix(half, 0)
    for w in range(wires):
        sorted_rows = jnp.dot(
            order, wire_refs[w][...], preferred_element_type=jnp.float32
        ).astype(jnp.bfloat16)
        for q in range(CUTS):
            place = (q, pl.ds(w * rows, rows))
            x_ref[place] = sorted_rows[q * rows : (q + 1) * rows]
            s_ref[place] = sorted_rows[(CUTS + q) * rows : (CUTS + q + 1) * rows]
    if last:

        @pl.when(taken)
        def _():
            turned = order_matrix(half, low)
            for w in range(wires):
                pltpu.make_async_copy(
                    slot_wires[w], picked_ref.at[w], sems.at[3 * CUTS + w]
                ).wait()
                picked = jnp.dot(
                    turned, picked_ref[w], preferred_element_type=jnp.float32
                ).astype(jnp.bfloat16)
                for q in range(CUTS):
                    place = (q, pl.ds(w * rows, rows))
                    picked_x_ref[place] = picked[q * rows : (q + 1) * rows]
                    picked_s_ref[place] = picked[(CUTS + q) * rows : (CUTS + q + 1) * rows]

        @pl.when(jnp.logical_not(taken))
        def _():
            picked_x_ref[...] = x_ref[...]
            picked_s_ref[...] = s_ref[...]

    total = wires * rows
    pre_gate = pre_up = d_hidden = jnp.zeros((total, hidden_width), jnp.float32)
    for q in range(CUTS):
        columns = pl.ds(q * quarter, quarter)
        for copy in copies[3 * q : 3 * q + 3]:
            copy.wait()
        for copy in copies[3 * (q + AHEAD) : 3 * (q + AHEAD) + 3]:
            copy.start()
        pre_gate += jnp.dot(x_ref[q], gate_ref[columns, :], preferred_element_type=jnp.float32)
        pre_up += jnp.dot(x_ref[q], up_ref[columns, :], preferred_element_type=jnp.float32)
        d_hidden += lax.dot_general(
            s_ref[q],
            down_ref[:, columns],
            (((1,), (1,)), ((), ())),
            preferred_element_type=jnp.float32,
        )
    sigma = 1.0 / (1.0 + jnp.exp(-pre_gate))
    active = pre_gate * sigma
    hidden = (active * pre_up).astype(jnp.bfloat16)
    d_gate = d_hidden * pre_up * sigma * (1.0 + pre_gate * (1.0 - sigma))
    acts_ref[:, :hidden_width] = hidden
    acts_ref[:, hidden_width : 2 * hidden_width] = d_gate.astype(jnp.bfloat16)
    acts_ref[:, 2 * hidden_width :] = (d_hidden * active).astype(jnp.bfloat16)
    score = jnp.sum(hidden.astype(jnp.float32) * d_hidden, axis=1, keepdims=True)
    row = lax.broadcasted_iota(jnp.int32, (total, 1), 0) % CAP
    lane = lax.broadcasted_iota(jnp.int32, (total, LANES), 1)
    spread = jnp.where(row == lane, score, 0.0)
    line = lax.broadcasted_iota(jnp.int32, (wires * half, 1), 0)
    group = (line // half) * rows + (line % half) * CAP
    member = lax.broadcasted_iota(jnp.int32, (wires * half, total), 1)
    scores = jnp.dot(
        jnp.where((member >= group) & (member < group + CAP), 1.0, 0.0),
        spread,
        precision=lax.Precision.HIGHEST,
        preferred_element_type=jnp.float32,
    )
    if last:
        for w in range(wires):
            part = slice(w * half, (w + 1) * half)
            first = 2 * half * ((plane_ref[0] - w + wires) % wires)
            near_rows = pl.ds(pl.multiple_of(first + half * side, half), half)
            far_rows = pl.ds(pl.multiple_of(first + half * (1 - side), half), half)
            score_ref[near_rows, :] = near_ref[part, :]
            score_ref[far_rows, :] = scores[part]
    else:
        score_ref[...] = scores


def home(wires, weights, half, *more):
    width, hidden_width = weights[0].shape
    count = len(wires)
    rows = count * half * CAP
    vmem = pl.BlockSpec(memory_space=pltpu.VMEM)
    hbm = pl.BlockSpec(memory_space=pltpu.HBM)
    smem = pl.BlockSpec(memory_space=pltpu.SMEM)
    parts = (CUTS, rows, width // CUTS)
    scratch = pltpu.VMEM(parts, jnp.bfloat16)
    out_shape = [
        jax.ShapeDtypeStruct((rows, 3 * hidden_width), jnp.bfloat16),
        jax.ShapeDtypeStruct((count * half * (2 if more else 1), LANES), jnp.float32),
    ]
    if more:
        out_shape += [jax.ShapeDtypeStruct(parts, jnp.bfloat16)] * 2
    return pl.pallas_call(
        functools.partial(home_kernel, half, count, bool(more)),
        out_shape=out_shape,
        in_specs=([smem, smem, smem, vmem] + [hbm] * count if more else []) + [vmem] * count + [hbm] * 3,
        out_specs=[vmem] * len(out_shape),
        scratch_shapes=([pltpu.VMEM((count,) + wires[0].shape, jnp.bfloat16)] if more else [])
        + [scratch, scratch]
        + [pltpu.VMEM(w.shape, jnp.bfloat16) for w in weights]
        + [pltpu.SemaphoreType.DMA((3 * CUTS + count,))],
        compiler_params=pltpu.CompilerParams(vmem_limit_bytes=56 * MIB),
        name="home_last" if more else "home",
    )(*more, *wires, *weights)


def sort_kernel(half, wires, slot_ref, flags_ref, *refs):
    known, refs = refs[:2], refs[2:]
    own_wires, slot_wires = refs[:wires], refs[wires : 2 * wires]
    x_ref, s_ref, wire_ref, sems = refs[2 * wires :]
    rows = half * CAP
    rest = [
        pltpu.make_async_copy(
            source, target.at[:, pl.ds(wires * rows, wires * rows), :], sems.at[wires + n]
        )
        for n, (source, target) in enumerate(zip(known, (x_ref, s_ref)))
    ]
    taken = flags_ref[slot_ref[0] % half] == 1

    def fetch(w, source):
        pltpu.make_async_copy(source, wire_ref.at[w], sems.at[w]).start()

    for w in range(wires):
        pl.when(taken)(functools.partial(fetch, w, slot_wires[w]))
        pl.when(jnp.logical_not(taken))(functools.partial(fetch, w, own_wires[w]))
    for copy in rest:
        copy.start()
    order = order_matrix(half, 0)
    for w in range(wires):
        pltpu.make_async_copy(own_wires[w], wire_ref.at[w], sems.at[w]).wait()
        sorted_rows = jnp.dot(order, wire_ref[w], preferred_element_type=jnp.float32).astype(
            jnp.bfloat16
        )
        for q in range(CUTS):
            x_ref[q, pl.ds(w * rows, rows), :] = sorted_rows[q * rows : (q + 1) * rows]
            s_ref[q, pl.ds(w * rows, rows), :] = sorted_rows[
                (CUTS + q) * rows : (CUTS + q + 1) * rows
            ]
    for copy in rest:
        copy.wait()


def sort_rows(slot, flags, known, own_wires, slot_wires, half):
    count = len(own_wires)
    quarter = own_wires[0].shape[1]
    rows = count * half * CAP
    vmem = pl.BlockSpec(memory_space=pltpu.VMEM)
    hbm = pl.BlockSpec(memory_space=pltpu.HBM)
    smem = pl.BlockSpec(memory_space=pltpu.SMEM)
    shape = jax.ShapeDtypeStruct((CUTS, 2 * rows, quarter), jnp.bfloat16)
    return pl.pallas_call(
        functools.partial(sort_kernel, half, count),
        out_shape=(shape, shape),
        in_specs=[smem, smem] + [hbm] * (2 + 2 * count),
        out_specs=(vmem, vmem),
        scratch_shapes=[
            pltpu.VMEM((count, half * BLOCK, quarter), jnp.bfloat16),
            pltpu.SemaphoreType.DMA((count + 2,)),
        ],
        compiler_params=params(((count,) + own_wires[0].shape, 2), (shape.shape, 2 * 2)),
        name="sort_rows",
    )(slot, flags, *known, *own_wires, *slot_wires)


def grads_kernel(half, parts, slot_ref, flags_ref, *refs):
    own_refs, other_refs = refs[:parts], refs[parts : 2 * parts]
    x_ref, s_ref, gate_ref, up_ref, down_ref, acts_ref, sems = refs[2 * parts :]
    rows = own_refs[0].shape[0]
    hidden_width = gate_ref.shape[1]

    @pl.when(pl.program_id(0) == 0)
    def _():
        taken = flags_ref[slot_ref[0] % half] == 1
        for p in range(parts):
            target = acts_ref.at[pl.ds(p * rows, rows), :]
            pl.when(taken)(pltpu.make_async_copy(other_refs[p], target, sems.at[p]).start)
            pl.when(jnp.logical_not(taken))(
                pltpu.make_async_copy(own_refs[p], target, sems.at[p]).start
            )
        for p in range(parts):
            target = acts_ref.at[pl.ds(p * rows, rows), :]
            pltpu.make_async_copy(own_refs[p], target, sems.at[p]).wait()

    contract = (((0,), (0,)), ((), ()))
    out = lax.dot_general(
        x_ref[0], acts_ref[:, hidden_width:], contract, preferred_element_type=jnp.float32
    )
    gate_ref[...] = out[:, :hidden_width].astype(jnp.bfloat16)
    up_ref[...] = out[:, hidden_width:].astype(jnp.bfloat16)
    down_ref[...] = lax.dot_general(
        acts_ref[:, :hidden_width], s_ref[0], contract, preferred_element_type=jnp.float32
    ).astype(jnp.bfloat16)


def grads(slot, flags, own, other, x_rows, s_rows, half):
    count = len(own)
    cuts, rows, quarter = x_rows.shape
    width = cuts * quarter
    triple = own[0].shape[1]
    hidden_width = triple // 3
    hbm = pl.BlockSpec(memory_space=pltpu.HBM)
    smem = pl.BlockSpec(memory_space=pltpu.SMEM)
    part = pl.BlockSpec((1, rows, quarter), lambda q: (q, 0, 0))
    return pl.pallas_call(
        functools.partial(grads_kernel, half, count),
        grid=(cuts,),
        out_shape=(
            jax.ShapeDtypeStruct((width, hidden_width), jnp.bfloat16),
            jax.ShapeDtypeStruct((width, hidden_width), jnp.bfloat16),
            jax.ShapeDtypeStruct((hidden_width, width), jnp.bfloat16),
        ),
        in_specs=[smem, smem] + [hbm] * (2 * count) + [part, part],
        out_specs=(
            pl.BlockSpec((quarter, hidden_width), lambda q: (q, 0)),
            pl.BlockSpec((quarter, hidden_width), lambda q: (q, 0)),
            pl.BlockSpec((hidden_width, quarter), lambda q: (0, q)),
        ),
        scratch_shapes=[
            pltpu.VMEM((rows, triple), jnp.bfloat16),
            pltpu.SemaphoreType.DMA((count,)),
        ],
        compiler_params=params(((rows, triple), 2), ((rows, quarter), 8), ((quarter, triple), 4)),
        name="grads",
    )(slot, flags, *own, *other, x_rows, s_rows)


def body(tokens, cotangent, expert_ids, gates, swap_flags, gate_w, up_w, down_w):
    axis_len = lax.axis_size("expert")
    planes = lax.axis_size("dp")
    half = axis_len // 2
    own_slot = lax.axis_index("expert")
    quarter = tokens.shape[1] // CUTS
    groups = [list(range(half)), list(range(half, axis_len))]
    slot = own_slot.reshape(1)
    plane = lax.axis_index("dp").reshape(1)

    def exchange(wire, name):
        with jax.named_scope(name):
            blocks = wire.reshape(half, BLOCK, quarter)
            moved = lax.all_to_all(
                blocks, "expert", split_axis=0, concat_axis=0, tiled=True, axis_index_groups=groups
            )
            return moved.reshape(half * BLOCK, quarter)

    def flip(block, by, name):
        with jax.named_scope(name):
            return lax.ppermute(block, "expert", [(i, i ^ by) for i in range(axis_len)])

    def across(block, name):
        return flip(block, half, name)

    def turned_exchange(mine, theirs, name, behind):
        pieces = []
        for c in range(half // 2):
            part = slice(c * BLOCK, (c + 1) * BLOCK)
            piece = jnp.concatenate([mine[part], theirs[part]], axis=0)
            pieces.append(flip(piece, 2 * c, name + str(c)) if c else piece)
        pieces = lax.optimization_barrier(tuple(pieces) + behind)[: half // 2]
        return jnp.concatenate(pieces, axis=0)

    def all_planes(wire, name):
        with jax.named_scope(name):
            return [wire] + [
                lax.ppermute(wire, "dp", [(i, (i + by) % planes) for i in range(planes)])
                for by in range(1, planes)
            ]

    def after(value, *others):
        return lax.optimization_barrier((value,) + others)[0]

    wire0, wire1, mine, theirs, pos = pack(
        slot, expert_ids.T, gates.T, tokens, cotangent, half
    )
    moved = across(wire1, "rows_across")
    theirs = flip(theirs, 1, "slot_rows_cores")
    home0 = exchange(wire0, "home_rows_half")
    homes0 = all_planes(home0, "home_rows_planes")
    slot1 = turned_exchange(mine, theirs, "slot_rows_chips", ())
    home1 = exchange(after(moved, slot1, *homes0[1:]), "crossed_rows_half")
    crossed = across(after(home0, slot1), "home_rows_across")
    slots1 = all_planes(slot1, "slot_rows_planes")
    homes1 = all_planes(home1, "crossed_rows_planes")
    homes1[0] = after(homes1[0], *slots1[1:])
    weights = (gate_w[0], up_w[0], down_w[0])
    acts0, score0 = home(homes0, weights, half)
    slots0 = all_planes(after(crossed, acts0), "slot_crossed_planes")
    acts1, back, x_rows1, s_rows1 = home(
        homes1, weights, half, slot, plane, swap_flags, score0, *slots1
    )
    own = [acts0, acts1]
    other = [across(acts0, "acts_near_across"), across(acts1, "acts_far_across")]
    x_rows, s_rows = sort_rows(slot, swap_flags, (x_rows1, s_rows1), homes0, slots0, half)

    returned = lax.all_to_all(
        back.reshape(planes * axis_len, 1, LANES),
        ("dp", "expert"),
        split_axis=0,
        concat_axis=0,
        tiled=True,
    )
    out_gate, out_up, out_down = grads(
        slot, swap_flags, own, other, x_rows, s_rows, half
    )
    returned = after(returned, out_down)
    total = jnp.sum(returned.reshape(planes, axis_len, LANES), axis=0)
    values = total[:, :CAP].reshape(-1)
    match = pos[:, :, None] == jnp.arange(axis_len * CAP, dtype=jnp.int32)[None, None, :]
    picked = jnp.sum(jnp.where(match, values[None, None, :], 0.0), axis=2)
    score_grad = (picked / gates.T.astype(jnp.float32)).T

    return (out_gate[None], out_up[None], out_down[None], score_grad)


def solution(mesh):
    placed = (
        P(("dp", "expert"), None),
        P(("dp", "expert"), None),
        P(("dp", "expert"), None),
        P(("dp", "expert"), None),
        P(),
        P("expert", None, "dp"),
        P("expert", None, "dp"),
        P("expert", "dp", None),
    )
    return jax.shard_map(
        body,
        mesh=mesh,
        in_specs=placed,
        out_specs=(
            P("expert", None, "dp"),
            P("expert", None, "dp"),
            P("expert", "dp", None),
            P(("dp", "expert"), None),
        ),
        check_vma=False,
    )
```
